32 devices in a mesh: row: 2 (over y), col: 4 (over x, core), layer: 4 (over z).
Axes of the slice: x: 2, y: 2, z: 4, core: 2. Of those that a mesh axis runs over, the one named last changes fastest.
Arguments:
- sign_iterate: bfloat16 [2048, 2048], P('row', 'col'), may hold values from -0.21875 to 0.21875
- square: bfloat16 [2048, 2048], P('row', 'col'), may hold values from -6 to 6
- pattern: int32 [16, 16], replicated, may hold values 0 or 1
- keep: int32 [16, 16], replicated, may hold values from 0 to 1, as said below
Outputs:
- product: bfloat16 [2048, 2048], P(('row', 'layer'), 'col')
The draws below stay inside these ranges and needn't reach their ends.
Inputs may be any that keep to these rules, and one draw needn't show every extreme that they name: In every region of 2 block rows by 4 block columns, aligned to the output's shards along row+layer and col, exactly 6 blocks have keep 1.
All inputs are finite; a program needn't handle non-finite values.
Results may differ from the reference program's by a relative error of at most 0.001.
Values may be sent and summed in bfloat16 or wider, within the bound.
A program may use at most 64 MiB of HBM per device.

```python
import jax
import jax.numpy as jnp

BLK = 128
ORDER = 2048
NB = 16
REGION_ROWS = 2
REGION_COLS = 4
KEPT = 6


def draw_keep(key, part):
    grid_rows = NB // REGION_ROWS
    grid_cols = NB // REGION_COLS
    count = REGION_ROWS * REGION_COLS
    subkey = jax.random.fold_in(key, 7)
    keys = jax.random.split(subkey, grid_rows * grid_cols)
    perms = jax.vmap(lambda k: jax.random.permutation(k, count))(keys)
    flags = (perms < KEPT).astype(jnp.int32)
    flags = flags.reshape(grid_rows, grid_cols, REGION_ROWS, REGION_COLS)
    return flags.transpose(0, 2, 1, 3).reshape(NB, NB)


def with_ends(entries, own_key, smallest, top_value):
    longest = entries.shape.index(max(entries.shape))
    spots = []
    for shift in (0, 1):
        where = [jax.random.randint(jax.random.fold_in(own_key, axis), (), 0, length) for axis, length in enumerate(entries.shape)]
        where[longest] = (where[longest] + shift) % entries.shape[longest]
        spots.append(tuple(where))
    return entries.at[spots[0]].set(smallest).at[spots[1]].set(top_value)


def levels(own_key, extent, cuts, low, top_value):
    def one(axis_at, blocks):
        draws = jax.random.uniform(jax.random.fold_in(jax.random.fold_in(own_key, 6), axis_at), (blocks,), jnp.float32, low / len(cuts), top_value / len(cuts))
        return jnp.repeat(jnp.exp(draws), extent[axis_at] // blocks).reshape((-1,) + (1,) * (len(extent) - axis_at - 1))

    factor_of = one(*cuts[0])
    for cut in cuts[1:]:
        factor_of = factor_of * one(*cut)
    return factor_of


def centred(stream_key, shape, scale, reach, cuts=(), kind=jnp.bfloat16):
    level = levels(stream_key, shape, cuts, -0.22, 0.18) if cuts else 1.0
    entries = jax.random.normal(stream_key, shape, jnp.float32) * scale * level
    return jnp.minimum(jnp.maximum(entries, -reach), reach).astype(kind)


def setup_inputs(seed: int = 0) -> dict:
    splits = jax.random.split(jax.random.key(seed), 5)
    sign_iterate = centred(splits[0], (ORDER, ORDER), (ORDER // 3) ** -0.5, 0.21875, ((0, 2), (1, 4)))
    square = centred(splits[1], (ORDER, ORDER), 1.0, 6.0, ((0, 2), (1, 4)))
    pattern = with_ends((jax.random.randint(splits[2], (NB, NB), 0, 3) < 1).astype(jnp.int32), jax.random.fold_in(splits[2], 1), 0, 1)
    keep = draw_keep(jax.random.fold_in(splits[4], 71), 0)
    return dict(sign_iterate=sign_iterate, square=square, pattern=pattern, keep=keep)


def apply_blocks(matrix, mask):
    nrow = mask.shape[0]
    ncol = mask.shape[1]
    shaped = matrix.reshape(nrow, BLK, ncol, BLK)
    chosen = (mask == 1)[:, None, :, None]
    return jnp.where(chosen, shaped, jnp.zeros_like(shaped)).reshape(matrix.shape)


def reference(sign_iterate, square, pattern, keep):
    stored = apply_blocks(sign_iterate, pattern)
    full = jnp.dot(stored, square, preferred_element_type=jnp.float32)
    return apply_blocks(full, keep).astype(jnp.bfloat16)
```

```python
import functools

import jax
import jax.numpy as jnp
from jax import lax
from jax.experimental import pallas as pl
from jax.experimental.pallas import tpu as pltpu
from jax.sharding import PartitionSpec as P

BLK = 128
GROUP = 256
PIECES = 4
MESH = pl.DeviceIdType.MESH


def kernel(
    n_row,
    n_col,
    n_layer,
    x_ref,
    s_ref,
    pattern_ref,
    keep_ref,
    o_ref,
    xbuf,
    xm,
    sbuf,
    acc,
    local_sem,
    y_send,
    y_recv,
    z_send,
    z_recv,
    x_send,
    x_recv,
    c_send,
    c_recv,
):
    row = lax.axis_index("row")
    col = lax.axis_index("col")
    layer = lax.axis_index("layer")
    _, m, kc = xbuf.shape
    _, sr, n = sbuf.shape
    n_group = sr // GROUP
    ch = GROUP // PIECES
    n_chunk = n_group * PIECES
    half = lax.rem(layer, 2)
    mate_layer = layer + 1 - 2 * half
    core = lax.rem(col, 2)
    mate_col = col + 1 - 2 * core
    n_chip = n_col // 2
    relayed = n_chunk // 2 - 1
    direct = n_chunk - relayed

    def peer_row(d):
        return lax.rem(row + d, n_row)

    def from_row(d):
        return lax.rem(row + n_row - d, n_row)

    def peer_col(e):
        return lax.rem(col + 2 * e, n_col)

    def from_col(e):
        return lax.rem(col + n_col - 2 * e, n_col)

    x_own = x_ref.at[pl.ds(pl.multiple_of(layer * m, m), m), :]
    copy_x = pltpu.make_async_copy(x_own, xbuf.at[col], local_sem.at[0])
    copy_s = pltpu.make_async_copy(s_ref, sbuf.at[row], local_sem.at[1])

    barrier = pltpu.get_barrier_semaphore()
    peers = [{"row": peer_row(d)} for d in range(1, n_row)]
    peers += [{"col": peer_col(e)} for e in range(1, n_chip)]
    peers += [{"layer": mate_layer}, {"col": mate_col}]
    for peer in peers:
        pl.semaphore_signal(barrier, inc=1, device_id=peer, device_id_type=MESH)
    copy_x.start()
    copy_s.start()
    pl.semaphore_wait(barrier, len(peers))

    def chunk_at(j, h):
        return pl.ds(pl.multiple_of((j + h * (n_chunk - 1 - 2 * j)) * ch, ch), ch)

    y = {}
    for j in range(direct):
        for d in range(1, n_row):
            rows = chunk_at(j, half)
            y[d, j] = pltpu.make_async_remote_copy(
                src_ref=s_ref.at[rows, :],
                dst_ref=sbuf.at[row, rows, :],
                send_sem=y_send.at[d - 1, j],
                recv_sem=y_recv.at[d - 1, j],
                device_id={"row": peer_row(d)},
                device_id_type=MESH,
            )
            y[d, j].start()
        if j == 0:
            xs = {}
            for e in range(1, n_chip):
                xs[e] = pltpu.make_async_remote_copy(
                    src_ref=x_own,
                    dst_ref=xbuf.at[col],
                    send_sem=x_send.at[e - 1],
                    recv_sem=x_recv.at[e - 1],
                    device_id={"col": peer_col(e)},
                    device_id_type=MESH,
                )
                xs[e].start()
            cs = {}
            cs[0] = pltpu.make_async_remote_copy(
                src_ref=x_own,
                dst_ref=xbuf.at[col],
                send_sem=c_send.at[0],
                recv_sem=c_recv.at[0],
                device_id={"col": mate_col},
                device_id_type=MESH,
            )
            cs[0].start()

    z = {}

    def land(j):
        for d in range(1, n_row):
            y[d, j].wait_recv()
            if j < relayed:
                place = sbuf.at[from_row(d), chunk_at(j, half), :]
                z[d, j] = pltpu.make_async_remote_copy(
                    src_ref=place,
                    dst_ref=place,
                    send_sem=z_send.at[d - 1, j],
                    recv_sem=z_recv.at[d - 1, j],
                    device_id={"layer": mate_layer},
                    device_id_type=MESH,
                )
                z[d, j].start()

    def pass_x():
        for e in range(1, n_chip):
            xs[e].wait_recv()
            place = xbuf.at[from_col(e)]
            cs[e] = pltpu.make_async_remote_copy(
                src_ref=place,
                dst_ref=place,
                send_sem=c_send.at[e],
                recv_sem=c_recv.at[e],
                device_id={"col": mate_col},
                device_id_type=MESH,
            )
            cs[e].start()

    first_row = (row * n_layer + layer) * (m // BLK)

    def mask_x():
        copy_x.wait()
        for e in range(n_chip):
            cs[e].wait_recv()
        for c in range(n_col):
            for a in range(m // BLK):
                for b in range(kc // BLK):
                    stored = pattern_ref[first_row + a, c * (kc // BLK) + b]
                    flags = jnp.full((BLK, BLK), stored, jnp.int32) == 1
                    piece = xbuf[c, a * BLK : (a + 1) * BLK, b * BLK : (b + 1) * BLK]
                    g, at = divmod(c * kc + b * BLK, GROUP)
                    xm[g, a * BLK : (a + 1) * BLK, at : at + BLK] = jnp.where(
                        flags, piece.astype(jnp.float32), 0.0
                    ).astype(jnp.bfloat16)

    def term(owner, g):
        rows = pl.ds(pl.multiple_of(g * GROUP, GROUP), GROUP)
        return jnp.dot(
            xm[owner * n_group + g], sbuf[owner, rows, :], preferred_element_type=jnp.float32
        )

    def group_of(i, h):
        return i + h * (n_group - 1 - 2 * i)

    done = 0
    x_passed = masked = False
    for j in range(direct):
        land(j)
        if j == direct // 2 - 1:
            pass_x()
            x_passed = True
        if j == direct // 2 + 1:
            mask_x()
            copy_s.wait()
            acc[...] = sum((term(row, g) for g in range(1, n_group)), term(row, 0))
            masked = True
        if x_passed and masked and j < direct - 1:
            while (done + 1) * PIECES <= j + 1:
                for d in range(1, n_row):
                    acc[...] += term(from_row(d), group_of(done, half))
                done += 1
    for i in range(n_group // 2 - 1):
        for d in range(1, n_row):
            for j in range(i * PIECES, (i + 1) * PIECES):
                z[d, j].wait_recv()
            acc[...] += term(from_row(d), group_of(i, 1 - half))
    last = n_group // 2 - 1
    for d in range(1, n_row):
        for j in range(last * PIECES, relayed):
            z[d, j].wait_recv()
        total = acc[...] + term(from_row(d), group_of(last, 1 - half))
        if d < n_row - 1:
            acc[...] = total

    for a in range(m // BLK):
        for b in range(n // BLK):
            kept = keep_ref[first_row + a, col * (n // BLK) + b]
            flags = jnp.full((BLK, BLK), kept, jnp.int32) == 1
            piece = total[a * BLK : (a + 1) * BLK, b * BLK : (b + 1) * BLK]
            o_ref[a * BLK : (a + 1) * BLK, b * BLK : (b + 1) * BLK] = jnp.where(
                flags, piece, 0.0
            ).astype(o_ref.dtype)

    for group in (y, z, xs, cs):
        for copy in group.values():
            copy.wait_send()


def shards(sign_iterate, square, pattern, keep):
    n_row, n_col, n_layer = (lax.axis_size(a) for a in ("row", "col", "layer"))
    rows, kc = sign_iterate.shape
    sr, n = square.shape
    m = rows // n_layer
    n_chunk = sr // GROUP * PIECES
    relayed = n_chunk // 2 - 1
    direct = n_chunk - relayed
    dma = pltpu.SemaphoreType.DMA
    order = n_col * kc
    return pl.pallas_call(
        functools.partial(kernel, n_row, n_col, n_layer),
        out_shape=jax.ShapeDtypeStruct((m, n), jnp.bfloat16),
        in_specs=[
            pl.BlockSpec(memory_space=pl.ANY),
            pl.BlockSpec(memory_space=pl.ANY),
            pl.BlockSpec(memory_space=pltpu.SMEM),
            pl.BlockSpec(memory_space=pltpu.SMEM),
        ],
        out_specs=pl.BlockSpec(memory_space=pltpu.VMEM),
        scratch_shapes=[
            pltpu.VMEM((n_col, m, kc), jnp.bfloat16),
            pltpu.VMEM((order // GROUP, m, GROUP), jnp.bfloat16),
            pltpu.VMEM((n_row, sr, n), jnp.bfloat16),
            pltpu.VMEM((m, n), jnp.float32),
            dma((2,)),
            dma((n_row - 1, direct)),
            dma((n_row - 1, direct)),
            dma((n_row - 1, relayed)),
            dma((n_row - 1, relayed)),
            dma((n_col // 2 - 1,)),
            dma((n_col // 2 - 1,)),
            dma((n_col // 2,)),
            dma((n_col // 2,)),
        ],
        compiler_params=pltpu.CompilerParams(
            collective_id=0, has_side_effects=True, vmem_limit_bytes=56 * 2**20
        ),
        cost_estimate=pl.CostEstimate(
            flops=2 * m * n * order,
            bytes_accessed=2 * (m * kc + sr * n + m * n),
            transcendentals=0,
        ),
    )(sign_iterate, square, pattern, keep)


def solution(mesh):
    return jax.shard_map(
        shards,
        mesh=mesh,
        in_specs=(P("row", "col"), P("row", "col"), P(), P()),
        out_specs=P(("row", "layer"), "col"),
        check_vma=False,
    )
```

```python
import functools

import jax
import jax.numpy as jnp
from jax import lax
from jax.experimental import pallas as pl
from jax.experimental.pallas import tpu as pltpu
from jax.sharding import PartitionSpec as P

BLK = 128
GROUP = 256
PIECES = 2
MESH = pl.DeviceIdType.MESH


def kernel(
    n_row,
    n_col,
    n_layer,
    x_ref,
    s_ref,
    pattern_hbm,
    keep_hbm,
    o_ref,
    pattern_ref,
    keep_ref,
    xbuf,
    xm,
    sbuf,
    acc,
    local_sem,
    y_send,
    y_recv,
    z_send,
    z_recv,
    x_send,
    x_recv,
    c_send,
    c_recv,
):
    row = lax.axis_index("row")
    col = lax.axis_index("col")
    layer = lax.axis_index("layer")
    _, m, kc = xbuf.shape
    _, sr, n = sbuf.shape
    n_group = sr // GROUP
    ch = GROUP // PIECES
    n_chunk = n_group * PIECES
    half = lax.rem(layer, 2)
    mate_layer = layer + 1 - 2 * half
    core = lax.rem(col, 2)
    mate_col = col + 1 - 2 * core
    n_chip = n_col // 2
    relayed = n_chunk // 2 - 1
    direct = n_chunk - relayed

    def peer_row(d):
        return lax.rem(row + d, n_row)

    def from_row(d):
        return lax.rem(row + n_row - d, n_row)

    def peer_col(e):
        return lax.rem(col + 2 * e, n_col)

    def from_col(e):
        return lax.rem(col + n_col - 2 * e, n_col)

    x_own = x_ref.at[pl.ds(pl.multiple_of(layer * m, m), m), :]
    copy_x = pltpu.make_async_copy(x_own, xbuf.at[col], local_sem.at[0])
    copy_s = pltpu.make_async_copy(s_ref, sbuf.at[row], local_sem.at[1])

    barrier = pltpu.get_barrier_semaphore()
    peers = [{"row": peer_row(d)} for d in range(1, n_row)]
    peers += [{"col": peer_col(e)} for e in range(1, n_chip)]
    peers += [{"layer": mate_layer}, {"col": mate_col}]
    for peer in peers:
        pl.semaphore_signal(barrier, inc=1, device_id=peer, device_id_type=MESH)
    copy_x.start()
    copy_s.start()
    copy_pattern = pltpu.make_async_copy(pattern_hbm, pattern_ref, local_sem.at[2])
    copy_keep = pltpu.make_async_copy(keep_hbm, keep_ref, local_sem.at[3])
    copy_pattern.start()
    copy_keep.start()
    pl.semaphore_wait(barrier, len(peers))

    def chunk_at(j, h):
        return pl.ds(pl.multiple_of((j + h * (n_chunk - 1 - 2 * j)) * ch, ch), ch)

    y = {}
    for j in range(direct):
        for d in range(1, n_row):
            rows = chunk_at(j, half)
            y[d, j] = pltpu.make_async_remote_copy(
                src_ref=s_ref.at[rows, :],
                dst_ref=sbuf.at[row, rows, :],
                send_sem=y_send.at[d - 1, j],
                recv_sem=y_recv.at[d - 1, j],
                device_id={"row": peer_row(d)},
                device_id_type=MESH,
            )
            y[d, j].start()
        if j == 0:
            xs = {}
            for e in range(1, n_chip):
                xs[e] = pltpu.make_async_remote_copy(
                    src_ref=x_own,
                    dst_ref=xbuf.at[col],
                    send_sem=x_send.at[e - 1],
                    recv_sem=x_recv.at[e - 1],
                    device_id={"col": peer_col(e)},
                    device_id_type=MESH,
                )
                xs[e].start()
            cs = {}
            cs[0] = pltpu.make_async_remote_copy(
                src_ref=x_own,
                dst_ref=xbuf.at[col],
                send_sem=c_send.at[0],
                recv_sem=c_recv.at[0],
                device_id={"col": mate_col},
                device_id_type=MESH,
            )
            cs[0].start()

    z = {}

    def land(j):
        for d in range(1, n_row):
            y[d, j].wait_recv()
            if j < relayed:
                place = sbuf.at[from_row(d), chunk_at(j, half), :]
                z[d, j] = pltpu.make_async_remote_copy(
                    src_ref=place,
                    dst_ref=place,
                    send_sem=z_send.at[d - 1, j],
                    recv_sem=z_recv.at[d - 1, j],
                    device_id={"layer": mate_layer},
                    device_id_type=MESH,
                )
                z[d, j].start()

    def pass_x():
        for e in range(1, n_chip):
            xs[e].wait_recv()
            place = xbuf.at[from_col(e)]
            cs[e] = pltpu.make_async_remote_copy(
                src_ref=place,
                dst_ref=place,
                send_sem=c_send.at[e],
                recv_sem=c_recv.at[e],
                device_id={"col": mate_col},
                device_id_type=MESH,
            )
            cs[e].start()

    first_row = (row * n_layer + layer) * (m // BLK)

    def mask_x():
        copy_x.wait()
        copy_pattern.wait()
        copy_keep.wait()
        for e in range(n_chip):
            cs[e].wait_recv()
        for c in range(n_col):
            for a in range(m // BLK):
                for b in range(kc // BLK):
                    stored = pattern_ref[first_row + a, c * (kc // BLK) + b]
                    flags = jnp.full((BLK, BLK), stored, jnp.int32) == 1
                    piece = xbuf[c, a * BLK : (a + 1) * BLK, b * BLK : (b + 1) * BLK]
                    g, at = divmod(c * kc + b * BLK, GROUP)
                    xm[g, a * BLK : (a + 1) * BLK, at : at + BLK] = jnp.where(
                        flags, piece.astype(jnp.float32), 0.0
                    ).astype(jnp.bfloat16)

    def term(owner, g):
        rows = pl.ds(pl.multiple_of(g * GROUP, GROUP), GROUP)
        return jnp.dot(
            xm[owner * n_group + g], sbuf[owner, rows, :], preferred_element_type=jnp.float32
        )

    def group_of(i, h):
        return i + h * (n_group - 1 - 2 * i)

    done = 0
    x_passed = masked = False
    for j in range(direct):
        land(j)
        if j == direct // 2 - 1:
            pass_x()
            x_passed = True
        if j == direct // 2 + 1:
            mask_x()
            copy_s.wait()
            acc[...] = sum((term(row, g) for g in range(1, n_group)), term(row, 0))
            masked = True
        if x_passed and masked and j < direct - 1:
            while (done + 1) * PIECES <= j + 1:
                for d in range(1, n_row):
                    acc[...] += term(from_row(d), group_of(done, half))
                done += 1
    for i in range(n_group // 2 - 1):
        for d in range(1, n_row):
            for j in range(i * PIECES, (i + 1) * PIECES):
                z[d, j].wait_recv()
            acc[...] += term(from_row(d), group_of(i, 1 - half))
    last = n_group // 2 - 1
    for d in range(1, n_row):
        for j in range(last * PIECES, relayed):
            z[d, j].wait_recv()
        total = acc[...] + term(from_row(d), group_of(last, 1 - half))
        if d < n_row - 1:
            acc[...] = total

    for a in range(m // BLK):
        for b in range(n // BLK):
            kept = keep_ref[first_row + a, col * (n // BLK) + b]
            flags = jnp.full((BLK, BLK), kept, jnp.int32) == 1
            piece = total[a * BLK : (a + 1) * BLK, b * BLK : (b + 1) * BLK]
            o_ref[a * BLK : (a + 1) * BLK, b * BLK : (b + 1) * BLK] = jnp.where(
                flags, piece, 0.0
            ).astype(o_ref.dtype)

    for group in (y, z, xs, cs):
        for copy in group.values():
            copy.wait_send()


def shards(sign_iterate, square, pattern, keep):
    n_row, n_col, n_layer = (lax.axis_size(a) for a in ("row", "col", "layer"))
    rows, kc = sign_iterate.shape
    sr, n = square.shape
    m = rows // n_layer
    n_chunk = sr // GROUP * PIECES
    relayed = n_chunk // 2 - 1
    direct = n_chunk - relayed
    dma = pltpu.SemaphoreType.DMA
    order = n_col * kc
    return pl.pallas_call(
        functools.partial(kernel, n_row, n_col, n_layer),
        out_shape=pltpu.VMEM((m, n), jnp.bfloat16),
        in_specs=[
            pl.BlockSpec(memory_space=pl.ANY),
            pl.BlockSpec(memory_space=pl.ANY),
            pl.BlockSpec(memory_space=pl.ANY),
            pl.BlockSpec(memory_space=pl.ANY),
        ],
        out_specs=pl.BlockSpec(memory_space=pltpu.VMEM),
        scratch_shapes=[
            pltpu.SMEM(pattern.shape, pattern.dtype),
            pltpu.SMEM(keep.shape, keep.dtype),
            pltpu.VMEM((n_col, m, kc), jnp.bfloat16),
            pltpu.VMEM((order // GROUP, m, GROUP), jnp.bfloat16),
            pltpu.VMEM((n_row, sr, n), jnp.bfloat16),
            pltpu.VMEM((m, n), jnp.float32),
            dma((4,)),
            dma((n_row - 1, direct)),
            dma((n_row - 1, direct)),
            dma((n_row - 1, relayed)),
            dma((n_row - 1, relayed)),
            dma((n_col // 2 - 1,)),
            dma((n_col // 2 - 1,)),
            dma((n_col // 2,)),
            dma((n_col // 2,)),
        ],
        compiler_params=pltpu.CompilerParams(
            collective_id=0, has_side_effects=True, vmem_limit_bytes=56 * 2**20
        ),
        cost_estimate=pl.CostEstimate(
            flops=2 * m * n * order,
            bytes_accessed=2 * (m * kc + sr * n + m * n),
            transcendentals=0,
        ),
    )(sign_iterate, square, pattern, keep)


def solution(mesh):
    return jax.shard_map(
        shards,
        mesh=mesh,
        in_specs=(P("row", "col"), P("row", "col"), P(), P()),
        out_specs=P(("row", "layer"), "col"),
        check_vma=False,
    )
```

```python
import functools

import jax
import jax.numpy as jnp
from jax import lax
from jax.experimental import pallas as pl
from jax.experimental.pallas import tpu as pltpu
from jax.sharding import PartitionSpec as P

BLK = 128
GROUP = 256
PIECES = 8
MESH = pl.DeviceIdType.MESH


def kernel(
    n_row,
    n_col,
    n_layer,
    x_ref,
    s_ref,
    pattern_hbm,
    keep_hbm,
    o_ref,
    pattern_ref,
    keep_ref,
    xbuf,
    xm,
    sbuf,
    acc,
    local_sem,
    y_send,
    y_recv,
    z_send,
    z_recv,
    x_send,
    x_recv,
    c_send,
    c_recv,
):
    row = lax.axis_index("row")
    col = lax.axis_index("col")
    layer = lax.axis_index("layer")
    _, m, kc = xbuf.shape
    _, sr, n = sbuf.shape
    n_group = sr // GROUP
    ch = GROUP // PIECES
    n_chunk = n_group * PIECES
    half = lax.rem(layer, 2)
    mate_layer = layer + 1 - 2 * half
    core = lax.rem(col, 2)
    mate_col = col + 1 - 2 * core
    n_chip = n_col // 2
    relayed = n_chunk // 2 - 3
    direct = n_chunk - relayed

    def peer_row(d):
        return lax.rem(row + d, n_row)

    def from_row(d):
        return lax.rem(row + n_row - d, n_row)

    def peer_col(e):
        return lax.rem(col + 2 * e, n_col)

    def from_col(e):
        return lax.rem(col + n_col - 2 * e, n_col)

    x_own = x_ref.at[pl.ds(pl.multiple_of(layer * m, m), m), :]
    copy_x = pltpu.make_async_copy(x_own, xbuf.at[col], local_sem.at[0])
    copy_s = pltpu.make_async_copy(s_ref, sbuf.at[row], local_sem.at[1])

    barrier = pltpu.get_barrier_semaphore()
    peers = [{"row": peer_row(d)} for d in range(1, n_row)]
    peers += [{"col": peer_col(e)} for e in range(1, n_chip)]
    peers += [{"layer": mate_layer}, {"col": mate_col}]
    for peer in peers:
        pl.semaphore_signal(barrier, inc=1, device_id=peer, device_id_type=MESH)
    copy_x.start()
    copy_s.start()
    copy_pattern = pltpu.make_async_copy(pattern_hbm, pattern_ref, local_sem.at[2])
    copy_keep = pltpu.make_async_copy(keep_hbm, keep_ref, local_sem.at[3])
    copy_pattern.start()
    copy_keep.start()
    pl.semaphore_wait(barrier, len(peers))
    copy_s.wait()

    def chunk_at(j, h):
        return pl.ds(pl.multiple_of((j + h * (n_chunk - 1 - 2 * j)) * ch, ch), ch)

    y = {}
    for j in range(direct):
        for d in range(1, n_row):
            rows = chunk_at(j, half)
            y[d, j] = pltpu.make_async_remote_copy(
                src_ref=sbuf.at[row, rows, :],
                dst_ref=sbuf.at[row, rows, :],
                send_sem=y_send.at[d - 1, j],
                recv_sem=y_recv.at[d - 1, j],
                device_id={"row": peer_row(d)},
                device_id_type=MESH,
            )
            y[d, j].start()
        if j == 0:
            xs = {}
            for e in range(1, n_chip):
                xs[e] = pltpu.make_async_remote_copy(
                    src_ref=x_own,
                    dst_ref=xbuf.at[col],
                    send_sem=x_send.at[e - 1],
                    recv_sem=x_recv.at[e - 1],
                    device_id={"col": peer_col(e)},
                    device_id_type=MESH,
                )
                xs[e].start()
            cs = {}
            cs[0] = pltpu.make_async_remote_copy(
                src_ref=x_own,
                dst_ref=xbuf.at[col],
                send_sem=c_send.at[0],
                recv_sem=c_recv.at[0],
                device_id={"col": mate_col},
                device_id_type=MESH,
            )
            cs[0].start()

    z = {}

    def land(j):
        for d in range(1, n_row):
            y[d, j].wait_recv()
            if j < relayed:
                place = sbuf.at[from_row(d), chunk_at(j, half), :]
                z[d, j] = pltpu.make_async_remote_copy(
                    src_ref=place,
                    dst_ref=place,
                    send_sem=z_send.at[d - 1, j],
                    recv_sem=z_recv.at[d - 1, j],
                    device_id={"layer": mate_layer},
                    device_id_type=MESH,
                )
                z[d, j].start()

    def pass_x():
        for e in range(1, n_chip):
            xs[e].wait_recv()
            place = xbuf.at[from_col(e)]
            cs[e] = pltpu.make_async_remote_copy(
                src_ref=place,
                dst_ref=place,
                send_sem=c_send.at[e],
                recv_sem=c_recv.at[e],
                device_id={"col": mate_col},
                device_id_type=MESH,
            )
            cs[e].start()

    first_row = (row * n_layer + layer) * (m // BLK)

    def mask_x():
        copy_x.wait()
        copy_pattern.wait()
        copy_keep.wait()
        for e in range(n_chip):
            cs[e].wait_recv()
        for c in range(n_col):
            for a in range(m // BLK):
                for b in range(kc // BLK):
                    stored = pattern_ref[first_row + a, c * (kc // BLK) + b]
                    flags = jnp.full((BLK, BLK), stored, jnp.int32) == 1
                    piece = xbuf[c, a * BLK : (a + 1) * BLK, b * BLK : (b + 1) * BLK]
                    g, at = divmod(c * kc + b * BLK, GROUP)
                    xm[g, a * BLK : (a + 1) * BLK, at : at + BLK] = jnp.where(
                        flags, piece.astype(jnp.float32), 0.0
                    ).astype(jnp.bfloat16)

    def term(owner, g):
        rows = pl.ds(pl.multiple_of(g * GROUP, GROUP), GROUP)
        return jnp.dot(
            xm[owner * n_group + g], sbuf[owner, rows, :], preferred_element_type=jnp.float32
        )

    def group_of(i, h):
        return i + h * (n_group - 1 - 2 * i)

    done = 0
    x_passed = masked = False
    for j in range(direct):
        land(j)
        if j == relayed - 3:
            pass_x()
            x_passed = True
        if j == relayed:
            mask_x()
            acc[...] = sum((term(row, g) for g in range(1, n_group)), term(row, 0))
            masked = True
        if x_passed and masked and j < direct - 1:
            while (done + 1) * PIECES <= j + 1:
                for d in range(1, n_row):
                    acc[...] += term(from_row(d), group_of(done, half))
                done += 1
    for i in range(n_group // 2 - 1):
        for d in range(1, n_row):
            for j in range(i * PIECES, (i + 1) * PIECES):
                z[d, j].wait_recv()
            acc[...] += term(from_row(d), group_of(i, 1 - half))
    last = n_group // 2 - 1
    for d in range(1, n_row):
        for j in range(last * PIECES, relayed):
            z[d, j].wait_recv()
        total = acc[...] + term(from_row(d), group_of(last, 1 - half))
        if d < n_row - 1:
            acc[...] = total

    for a in range(m // BLK):
        for b in range(n // BLK):
            kept = keep_ref[first_row + a, col * (n // BLK) + b]
            flags = jnp.full((BLK, BLK), kept, jnp.int32) == 1
            piece = total[a * BLK : (a + 1) * BLK, b * BLK : (b + 1) * BLK]
            o_ref[a * BLK : (a + 1) * BLK, b * BLK : (b + 1) * BLK] = jnp.where(
                flags, piece, 0.0
            ).astype(o_ref.dtype)

    for group in (y, z, xs, cs):
        for copy in group.values():
            copy.wait_send()


def shards(sign_iterate, square, pattern, keep):
    n_row, n_col, n_layer = (lax.axis_size(a) for a in ("row", "col", "layer"))
    rows, kc = sign_iterate.shape
    sr, n = square.shape
    m = rows // n_layer
    n_chunk = sr // GROUP * PIECES
    relayed = n_chunk // 2 - 3
    direct = n_chunk - relayed
    dma = pltpu.SemaphoreType.DMA
    order = n_col * kc
    return pl.pallas_call(
        functools.partial(kernel, n_row, n_col, n_layer),
        out_shape=pltpu.VMEM((m, n), jnp.bfloat16),
        in_specs=[
            pl.BlockSpec(memory_space=pl.ANY),
            pl.BlockSpec(memory_space=pl.ANY),
            pl.BlockSpec(memory_space=pl.ANY),
            pl.BlockSpec(memory_space=pl.ANY),
        ],
        out_specs=pl.BlockSpec(memory_space=pltpu.VMEM),
        scratch_shapes=[
            pltpu.SMEM(pattern.shape, pattern.dtype),
            pltpu.SMEM(keep.shape, keep.dtype),
            pltpu.VMEM((n_col, m, kc), jnp.bfloat16),
            pltpu.VMEM((order // GROUP, m, GROUP), jnp.bfloat16),
            pltpu.VMEM((n_row, sr, n), jnp.bfloat16),
            pltpu.VMEM((m, n), jnp.float32),
            dma((4,)),
            dma((n_row - 1, direct)),
            dma((n_row - 1, direct)),
            dma((n_row - 1, relayed)),
            dma((n_row - 1, relayed)),
            dma((n_col // 2 - 1,)),
            dma((n_col // 2 - 1,)),
            dma((n_col // 2,)),
            dma((n_col // 2,)),
        ],
        compiler_params=pltpu.CompilerParams(
            collective_id=0, has_side_effects=True, vmem_limit_bytes=56 * 2**20
        ),
        cost_estimate=pl.CostEstimate(
            flops=2 * m * n * order,
            bytes_accessed=2 * (m * kc + sr * n + m * n),
            transcendentals=0,
        ),
    )(sign_iterate, square, pattern, keep)


def solution(mesh):
    return jax.shard_map(
        shards,
        mesh=mesh,
        in_specs=(P("row", "col"), P("row", "col"), P(), P()),
        out_specs=P(("row", "layer"), "col"),
        check_vma=False,
    )
```

```python
import functools

import jax
import jax.numpy as jnp
from jax import lax
from jax.experimental import pallas as pl
from jax.experimental.pallas import tpu as pltpu
from jax.sharding import PartitionSpec as P

BLK = 128
GROUP = 256
PIECES = 8
MESH = pl.DeviceIdType.MESH


def kernel(
    n_row,
    n_col,
    n_layer,
    x_ref,
    s_ref,
    pattern_hbm,
    keep_hbm,
    o_ref,
    pattern_ref,
    keep_ref,
    xbuf,
    xm,
    sbuf,
    acc,
    local_sem,
    y_send,
    y_recv,
    z_send,
    z_recv,
    x_send,
    x_recv,
    c_send,
    c_recv,
):
    row = lax.axis_index("row")
    col = lax.axis_index("col")
    layer = lax.axis_index("layer")
    _, m, kc = xbuf.shape
    _, sr, n = sbuf.shape
    n_group = sr // GROUP
    ch = GROUP // PIECES
    n_chunk = n_group * PIECES
    half = lax.rem(layer, 2)
    mate_layer = layer + 1 - 2 * half
    core = lax.rem(col, 2)
    mate_col = col + 1 - 2 * core
    n_chip = n_col // 2
    relayed = n_chunk // 2 - 3
    direct = relayed + 1
    tail = pl.ds(relayed * ch, (n_chunk - 2 * relayed) * ch)

    def peer_row(d):
        return lax.rem(row + d, n_row)

    def from_row(d):
        return lax.rem(row + n_row - d, n_row)

    def peer_col(e):
        return lax.rem(col + 2 * e, n_col)

    def from_col(e):
        return lax.rem(col + n_col - 2 * e, n_col)

    x_own = x_ref.at[pl.ds(pl.multiple_of(layer * m, m), m), :]
    copy_x = pltpu.make_async_copy(x_own, xbuf.at[col], local_sem.at[0])
    copy_s = pltpu.make_async_copy(s_ref, sbuf.at[row], local_sem.at[1])

    barrier = pltpu.get_barrier_semaphore()
    peers = [{"row": peer_row(d)} for d in range(1, n_row)]
    peers += [{"col": peer_col(e)} for e in range(1, n_chip)]
    peers += [{"layer": mate_layer}, {"col": mate_col}]
    for peer in peers:
        pl.semaphore_signal(barrier, inc=1, device_id=peer, device_id_type=MESH)
    copy_x.start()
    copy_s.start()
    copy_pattern = pltpu.make_async_copy(pattern_hbm, pattern_ref, local_sem.at[2])
    copy_keep = pltpu.make_async_copy(keep_hbm, keep_ref, local_sem.at[3])
    copy_pattern.start()
    copy_keep.start()
    pl.semaphore_wait(barrier, len(peers))
    copy_s.wait()

    def chunk_at(j, h):
        return pl.ds(pl.multiple_of((j + h * (n_chunk - 1 - 2 * j)) * ch, ch), ch)

    y = {}
    for j in range(direct):
        for d in range(1, n_row):
            rows = chunk_at(j, half) if j < relayed else tail
            y[d, j] = pltpu.make_async_remote_copy(
                src_ref=sbuf.at[row, rows, :],
                dst_ref=sbuf.at[row, rows, :],
                send_sem=y_send.at[d - 1, j],
                recv_sem=y_recv.at[d - 1, j],
                device_id={"row": peer_row(d)},
                device_id_type=MESH,
            )
            y[d, j].start()
        if j == 0:
            xs = {}
            for e in range(1, n_chip):
                xs[e] = pltpu.make_async_remote_copy(
                    src_ref=x_own,
                    dst_ref=xbuf.at[col],
                    send_sem=x_send.at[e - 1],
                    recv_sem=x_recv.at[e - 1],
                    device_id={"col": peer_col(e)},
                    device_id_type=MESH,
                )
                xs[e].start()
            cs = {}
            cs[0] = pltpu.make_async_remote_copy(
                src_ref=x_own,
                dst_ref=xbuf.at[col],
                send_sem=c_send.at[0],
                recv_sem=c_recv.at[0],
                device_id={"col": mate_col},
                device_id_type=MESH,
            )
            cs[0].start()

    z = {}

    def land(j):
        for d in range(1, n_row):
            y[d, j].wait_recv()
            if j < relayed:
                place = sbuf.at[from_row(d), chunk_at(j, half), :]
                z[d, j] = pltpu.make_async_remote_copy(
                    src_ref=place,
                    dst_ref=place,
                    send_sem=z_send.at[d - 1, j],
                    recv_sem=z_recv.at[d - 1, j],
                    device_id={"layer": mate_layer},
                    device_id_type=MESH,
                )
                z[d, j].start()

    def pass_x():
        for e in range(1, n_chip):
            xs[e].wait_recv()
            place = xbuf.at[from_col(e)]
            cs[e] = pltpu.make_async_remote_copy(
                src_ref=place,
                dst_ref=place,
                send_sem=c_send.at[e],
                recv_sem=c_recv.at[e],
                device_id={"col": mate_col},
                device_id_type=MESH,
            )
            cs[e].start()

    first_row = (row * n_layer + layer) * (m // BLK)

    def mask_x():
        copy_x.wait()
        copy_pattern.wait()
        copy_keep.wait()
        for e in range(n_chip):
            cs[e].wait_recv()
        for c in range(n_col):
            for a in range(m // BLK):
                for b in range(kc // BLK):
                    stored = pattern_ref[first_row + a, c * (kc // BLK) + b]
                    flags = jnp.full((BLK, BLK), stored, jnp.int32) == 1
                    piece = xbuf[c, a * BLK : (a + 1) * BLK, b * BLK : (b + 1) * BLK]
                    g, at = divmod(c * kc + b * BLK, GROUP)
                    xm[g, a * BLK : (a + 1) * BLK, at : at + BLK] = jnp.where(
                        flags, piece.astype(jnp.float32), 0.0
                    ).astype(jnp.bfloat16)

    def term(owner, g):
        rows = pl.ds(pl.multiple_of(g * GROUP, GROUP), GROUP)
        return jnp.dot(
            xm[owner * n_group + g], sbuf[owner, rows, :], preferred_element_type=jnp.float32
        )

    def group_of(i, h):
        return i + h * (n_group - 1 - 2 * i)

    done = 0
    x_passed = masked = False
    for j in range(direct):
        land(j)
        if j == relayed - 3:
            pass_x()
            x_passed = True
        if j == relayed - 1:
            mask_x()
            acc[...] = sum((term(row, g) for g in range(1, n_group)), term(row, 0))
            masked = True
        if x_passed and masked and j < direct - 1:
            while (done + 1) * PIECES <= j + 1:
                for d in range(1, n_row):
                    acc[...] += term(from_row(d), group_of(done, half))
                done += 1
    for i in range(done, n_group // 2):
        for d in range(1, n_row):
            acc[...] += term(from_row(d), group_of(i, half))
    for i in range(n_group // 2 - 1):
        for d in range(1, n_row):
            for j in range(i * PIECES, (i + 1) * PIECES):
                z[d, j].wait_recv()
            acc[...] += term(from_row(d), group_of(i, 1 - half))
    last = n_group // 2 - 1
    for d in range(1, n_row):
        for j in range(last * PIECES, relayed):
            z[d, j].wait_recv()
        total = acc[...] + term(from_row(d), group_of(last, 1 - half))
        if d < n_row - 1:
            acc[...] = total

    for a in range(m // BLK):
        for b in range(n // BLK):
            kept = keep_ref[first_row + a, col * (n // BLK) + b]
            flags = jnp.full((BLK, BLK), kept, jnp.int32) == 1
            piece = total[a * BLK : (a + 1) * BLK, b * BLK : (b + 1) * BLK]
            o_ref[a * BLK : (a + 1) * BLK, b * BLK : (b + 1) * BLK] = jnp.where(
                flags, piece, 0.0
            ).astype(o_ref.dtype)

    for group in (y, z, xs, cs):
        for copy in group.values():
            copy.wait_send()


def shards(sign_iterate, square, pattern, keep):
    n_row, n_col, n_layer = (lax.axis_size(a) for a in ("row", "col", "layer"))
    rows, kc = sign_iterate.shape
    sr, n = square.shape
    m = rows // n_layer
    n_chunk = sr // GROUP * PIECES
    relayed = n_chunk // 2 - 3
    direct = relayed + 1
    dma = pltpu.SemaphoreType.DMA
    order = n_col * kc
    return pl.pallas_call(
        functools.partial(kernel, n_row, n_col, n_layer),
        out_shape=pltpu.VMEM((m, n), jnp.bfloat16),
        in_specs=[
            pl.BlockSpec(memory_space=pl.ANY),
            pl.BlockSpec(memory_space=pl.ANY),
            pl.BlockSpec(memory_space=pl.ANY),
            pl.BlockSpec(memory_space=pl.ANY),
        ],
        out_specs=pl.BlockSpec(memory_space=pltpu.VMEM),
        scratch_shapes=[
            pltpu.SMEM(pattern.shape, pattern.dtype),
            pltpu.SMEM(keep.shape, keep.dtype),
            pltpu.VMEM((n_col, m, kc), jnp.bfloat16),
            pltpu.VMEM((order // GROUP, m, GROUP), jnp.bfloat16),
            pltpu.VMEM((n_row, sr, n), jnp.bfloat16),
            pltpu.VMEM((m, n), jnp.float32),
            dma((4,)),
            dma((n_row - 1, direct)),
            dma((n_row - 1, direct)),
            dma((n_row - 1, relayed)),
            dma((n_row - 1, relayed)),
            dma((n_col // 2 - 1,)),
            dma((n_col // 2 - 1,)),
            dma((n_col // 2,)),
            dma((n_col // 2,)),
        ],
        compiler_params=pltpu.CompilerParams(
            collective_id=0, has_side_effects=True, vmem_limit_bytes=56 * 2**20
        ),
        cost_estimate=pl.CostEstimate(
            flops=2 * m * n * order,
            bytes_accessed=2 * (m * kc + sr * n + m * n),
            transcendentals=0,
        ),
    )(sign_iterate, square, pattern, keep)


def solution(mesh):
    return jax.shard_map(
        shards,
        mesh=mesh,
        in_specs=(P("row", "col"), P("row", "col"), P(), P()),
        out_specs=P(("row", "layer"), "col"),
        check_vma=False,
    )
```
